32 devices in a mesh: orbit: 8 (over z, core), space: 4 (over y, x).
Axes of the slice: x: 2, y: 2, z: 4, core: 2. Of those that a mesh axis runs over, the one named last changes fastest.
Arguments:
- queries: bfloat16 [8, 8, 64, 2240], P('orbit', 'space'), may hold values from -6 to 6
- keys_in: bfloat16 [8, 8, 64, 2240], P('orbit', 'space'), may hold values from -6 to 6
- values: bfloat16 [8, 8, 64, 2240], P('orbit', 'space'), may hold values from -6 to 6
- conv_weight: bfloat16 [3, 3, 2240], replicated, may hold values from -2 to 2
- grad_out: bfloat16 [8, 8, 64, 2240], P('orbit', 'space'), may hold values from -6 to 6
Outputs:
- attended: bfloat16 [8, 8, 64, 2240], P('orbit', 'space')
- grad_query: bfloat16 [8, 8, 64, 2240], P('orbit', 'space')
- grad_key: bfloat16 [8, 8, 64, 2240], P('orbit', 'space')
- grad_value: bfloat16 [8, 8, 64, 2240], P('orbit', 'space')
The draws below stay inside these ranges and needn't reach their ends.
All inputs are finite; a program needn't handle non-finite values.
Results may differ from the reference program's by a relative error of at most 0.0079.
Values may be sent and summed in bfloat16 or wider, within the bound.
A program may use at most 128 MiB of HBM per device.

```python
import math
import jax
import jax.numpy as jnp
from jax import lax

HEADS = 20
HD = 112
D = 2240
COLS = 64
LROWS = 8
VIEWS = 8


def offset_field(key, view_scale, row_scale):
    key_base, second, last_key = jax.random.split(key, 3)
    field_shape = (VIEWS, LROWS, COLS, D)
    base_field = jax.random.normal(key_base, field_shape, jnp.float32)
    view_offset = jax.random.normal(second, (VIEWS, 1, 1, D), jnp.float32) * view_scale
    row_offset = jax.random.normal(last_key, (VIEWS, LROWS, 1, D), jnp.float32) * row_scale
    return jnp.clip(base_field + view_offset + row_offset, -6.0, 6.0)


def draw_queries(key, part):
    key = jax.random.fold_in(key, 101)
    key_base, second = jax.random.split(key)
    field_shape = (VIEWS, LROWS, COLS, HEADS, HD)
    base_field = jax.random.normal(key_base, field_shape, jnp.float32)
    spread = jnp.exp(jax.random.uniform(second, (VIEWS, LROWS, COLS, HEADS, 1), jnp.float32, math.log(0.02), math.log(1.5)))
    return jnp.clip(base_field * spread, -6.0, 6.0).reshape(VIEWS, LROWS, COLS, D).astype(jnp.bfloat16)


def draw_keys_in(key, part):
    return offset_field(jax.random.fold_in(key, 202), 0.7, 0.4).astype(jnp.bfloat16)


def draw_values(key, part):
    return offset_field(jax.random.fold_in(key, 303), 1.0, 0.6).astype(jnp.bfloat16)


def draw_grad_out(key, part):
    return offset_field(jax.random.fold_in(key, 404), 0.8, 0.5).astype(jnp.bfloat16)


def centred(rng, shape, scale, bound, held_as=jnp.bfloat16):
    return jnp.clip(scale * jax.random.normal(rng, shape, jnp.float32), -bound, bound).astype(held_as)


def setup_inputs(seed: int = 0) -> dict:
    splits = jax.random.split(jax.random.key(seed), 6)
    return {
        "queries": draw_queries(jax.random.fold_in(splits[5], 71), 0),
        "keys_in": draw_keys_in(jax.random.fold_in(splits[5], 71), 0),
        "values": draw_values(jax.random.fold_in(splits[5], 71), 0),
        "conv_weight": centred(splits[3], (3, 3, D), 9 ** -0.5, 2.0),
        "grad_out": draw_grad_out(jax.random.fold_in(splits[5], 71), 0),
    }


def conv_apply(source_field, conv_weight):
    padded = jnp.pad(source_field.astype(jnp.float32), ((1, 1), (1, 1), (0, 0)))
    weight_wide = conv_weight.astype(jnp.float32)
    running_sum = jnp.zeros(source_field.shape, jnp.float32)
    for row_step in range(3):
        for col_step in range(3):
            running_sum = running_sum + weight_wide[row_step, col_step] * padded[row_step:row_step + LROWS, col_step:col_step + COLS]
    return running_sum


def conv_back(source_field, conv_weight):
    padded = jnp.pad(source_field.astype(jnp.float32), ((1, 1), (1, 1), (0, 0)))
    weight_wide = conv_weight.astype(jnp.float32)
    running_sum = jnp.zeros(source_field.shape, jnp.float32)
    for row_step in range(3):
        for col_step in range(3):
            running_sum = running_sum + weight_wide[row_step, col_step] * padded[2 - row_step:2 - row_step + LROWS, 2 - col_step:2 - col_step + COLS]
    return running_sum


def reference(queries, keys_in, values, conv_weight, grad_out):
    token_count = LROWS * COLS
    heads_shape = (token_count, HEADS, HD)
    counts = (jnp.arange(VIEWS, dtype=jnp.float32) + 1.0) * float(token_count)

    def local_state(pair_items):
        key_view, value_view = pair_items
        key_feat = jax.nn.relu(key_view).reshape(heads_shape).astype(jnp.float32)
        value_heads = value_view.reshape(heads_shape).astype(jnp.float32)
        state_part = jnp.einsum("thd,the->hde", key_feat, value_heads)
        norm_part = jnp.sum(key_feat, axis=0)
        return state_part, norm_part

    state_parts, norm_parts = lax.map(local_state, (keys_in, values))
    state_b = (jnp.cumsum(state_parts, 0) / counts[:, None, None, None]).astype(jnp.bfloat16)
    norm_b = (jnp.cumsum(norm_parts, 0) / counts[:, None, None]).astype(jnp.bfloat16)

    def forward_view(view_items):
        query_view, value_view, grad_view, state_view, norm_view = view_items
        query_feat = jax.nn.relu(query_view).reshape(heads_shape).astype(jnp.float32)
        state_wide = state_view.astype(jnp.float32)
        norm_wide = norm_view.astype(jnp.float32)
        numerator = jnp.einsum("thd,hde->the", query_feat, state_wide)
        denominator = jnp.einsum("thd,hd->th", query_feat, norm_wide) + 1.0
        attention = numerator / denominator[..., None]
        attended = (attention.reshape(LROWS, COLS, HEADS * HD) + conv_apply(value_view, conv_weight)).astype(jnp.bfloat16)
        grad_wide = grad_view.reshape(heads_shape).astype(jnp.float32)
        numerator_grad = (grad_wide / denominator[..., None]).astype(jnp.bfloat16).astype(jnp.float32)
        denominator_grad = (-jnp.sum(grad_wide * numerator, -1) / (denominator * denominator)).astype(jnp.bfloat16).astype(jnp.float32)
        query_grad = jnp.einsum("the,hde->thd", numerator_grad, state_wide) + denominator_grad[..., None] * norm_wide[None]
        grad_query = jnp.where(query_view.reshape(heads_shape) > 0, query_grad, 0.0).astype(jnp.bfloat16).reshape(LROWS, COLS, HEADS * HD)
        state_grad = jnp.einsum("thd,the->hde", query_feat, numerator_grad)
        norm_grad = jnp.einsum("thd,th->hd", query_feat, denominator_grad)
        return attended, grad_query, state_grad, norm_grad

    attended, grad_query, state_grads, norm_grads = lax.map(forward_view, (queries, values, grad_out, state_b, norm_b))
    scaled_state = state_grads / counts[:, None, None, None]
    scaled_norm = norm_grads / counts[:, None, None]
    back_state = jnp.flip(jnp.cumsum(jnp.flip(scaled_state, 0), 0), 0).astype(jnp.bfloat16)
    back_norm = jnp.flip(jnp.cumsum(jnp.flip(scaled_norm, 0), 0), 0).astype(jnp.bfloat16)

    def backward_view(view_items):
        key_view, value_view, grad_view, state_view, norm_view = view_items
        key_feat = jax.nn.relu(key_view).reshape(heads_shape).astype(jnp.float32)
        value_heads = value_view.reshape(heads_shape).astype(jnp.float32)
        state_wide = state_view.astype(jnp.float32)
        key_grad = jnp.einsum("the,hde->thd", value_heads, state_wide) + norm_view.astype(jnp.float32)[None]
        grad_key = jnp.where(key_view.reshape(heads_shape) > 0, key_grad, 0.0).astype(jnp.bfloat16).reshape(LROWS, COLS, HEADS * HD)
        value_grad = jnp.einsum("thd,hde->the", key_feat, state_wide).reshape(LROWS, COLS, HEADS * HD) + conv_back(grad_view, conv_weight)
        return grad_key, value_grad.astype(jnp.bfloat16)

    grad_key, grad_value = lax.map(backward_view, (keys_in, values, grad_out, back_state, back_norm))
    return (attended, grad_query, grad_key, grad_value)
```

```python
import functools
import math

import jax
import jax.numpy as jnp
from jax import lax
from jax.experimental import pallas as pl
from jax.experimental.pallas import tpu as pltpu
from jax.sharding import PartitionSpec as P

HEADS = 20
HD = 112
LANES = 128
GROUP = 4
GROUPS = HEADS // GROUP
BF = jnp.bfloat16
F32 = jnp.float32
MESH = pl.DeviceIdType.MESH


def dot_tn(a, b):
    return lax.dot_general(a, b, (((0,), (0,)), ((), ())), preferred_element_type=F32)


def dot_nt(a, b):
    return lax.dot_general(a, b, (((1,), (1,)), ((), ())), preferred_element_type=F32)


def dot_nn(a, b):
    return lax.dot_general(a, b, (((1,), (0,)), ((), ())), preferred_element_type=F32)


def kernel(
    nz, n1, n2, chunk,
    q_ref, k_ref, v_ref, w_ref, g_ref,
    att_ref, gq_ref, gk_ref, gv_ref,
    vx, kx, gx, att32, gq32, gk32, gv32, halo_v, halo_g,
    st32, st16, a32, a16, p32, t16, rs1, rs2, pc, zr, full,
    halo_ss, halo_rs, rs1_ss, rs1_rs, rs2_ss, rs2_rs, pc_ss, pc_rs, zr_ss, zr_rs,
    agx_ss, agx_rs, agy_ss, agy_rs,
):
    rows, cols, width = v_ref.shape
    tokens = rows * cols
    n = n1 * n2
    wide = n2 * chunk
    group_rows = GROUP * HD
    u = lax.axis_index("orbit")
    s = lax.axis_index("space")
    z, core = u // 2, u % 2
    y, x = s // n2, s % n2
    count = (u + 1).astype(F32) * float(rows * n * cols)
    inv_count = 1.0 / count
    pair = z * 2 + (1 - core)

    def y_peer(k):
        return {"space": lax.rem(y + k, n1) * n2 + x}

    def x_peer(k):
        return {"space": y * n2 + lax.rem(x + k, n2)}

    def z_peer(k):
        return {"orbit": (z + k) * 2 + core}

    barrier = pltpu.get_barrier_semaphore()
    for k in range(1, n1):
        pl.semaphore_signal(barrier, inc=1, device_id=y_peer(k), device_id_type=MESH)
    for k in range(1, n2):
        pl.semaphore_signal(barrier, inc=1, device_id=x_peer(k), device_id_type=MESH)
    pl.semaphore_signal(barrier, inc=1, device_id={"orbit": pair}, device_id_type=MESH)
    for k in range(1, nz):
        pl.semaphore_signal(
            barrier, inc=1, device_id={"orbit": lax.rem(z + k, nz) * 2 + core},
            device_id_type=MESH,
        )

    @pl.when(s > 0)
    def _():
        pl.semaphore_signal(barrier, inc=1, device_id={"space": s - 1}, device_id_type=MESH)

    @pl.when(s < n - 1)
    def _():
        pl.semaphore_signal(barrier, inc=1, device_id={"space": s + 1}, device_id_type=MESH)

    lane = lax.broadcasted_iota(jnp.int32, (tokens, LANES), 1)
    ones_column = jnp.where(lane == HD, 1.0, 0.0).astype(BF)
    zero_block = jnp.zeros((tokens, LANES), BF)

    def columns(h):
        return slice(h * HD, (h + 1) * HD)

    def flat(ref, where):
        return ref[:, :, where].reshape(tokens, -1)

    def put_state(ph, g, j, block):
        st32[ph, g, j * HD:(j + 1) * HD] = block
        st16[ph, g, j * HD:(j + 1) * HD] = block.astype(BF)

    def pad_state(ph, g):
        if n * chunk > group_rows:
            extra = n * chunk - group_rows
            st32[ph, g, group_rows:] = jnp.zeros((extra, LANES), F32)
            st16[ph, g, group_rows:] = jnp.zeros((extra, LANES), BF)

    def remote(src, dst, ss, rs, to):
        return pltpu.make_async_remote_copy(
            src_ref=src, dst_ref=dst, send_sem=ss, recv_sem=rs,
            device_id=to, device_id_type=MESH,
        )

    def copy_rs1(ph, g, k):
        part = st16.at[ph, g, pl.ds(lax.rem(y + k, n1) * wide, wide)]
        i = (ph, g, k - 1)
        return remote(part, rs1.at[i], rs1_ss.at[i], rs1_rs.at[i], y_peer(k))

    def copy_rs2(ph, g, k):
        part = a16.at[ph, g, pl.ds(lax.rem(x + k, n2) * chunk, chunk)]
        i = (ph, g, k - 1)
        return remote(part, rs2.at[i], rs2_ss.at[i], rs2_rs.at[i], x_peer(k))

    def copy_pc(ph, g):
        i = (ph, g)
        return remote(p32.at[i], pc.at[i], pc_ss.at[i], pc_rs.at[i], {"orbit": pair})

    def copy_zr(ph, g, k):
        i = (ph, g, k - 1)
        return remote(
            t16.at[ph, g], zr.at[i], zr_ss.at[i], zr_rs.at[i], z_peer(k if ph == 0 else -k)
        )

    def z_sends(ph, k):
        return (z + k < nz) if ph == 0 else (z - k >= 0)

    def z_gets(ph, k):
        return (z - k >= 0) if ph == 0 else (z + k < nz)

    def copy_agx(ph, g, k):
        i = (ph, g, k - 1)
        here = full.at[ph, g, pl.ds(s * chunk, chunk)]
        return remote(here, here, agx_ss.at[i], agx_rs.at[i], x_peer(k))

    def got_agx(ph, g, k):
        i = (ph, g, k - 1)
        there = full.at[ph, g, pl.ds((y * n2 + lax.rem(x + n2 - k, n2)) * chunk, chunk)]
        return remote(there, there, agx_ss.at[i], agx_rs.at[i], x_peer(k))

    def copy_agy(ph, g, k):
        i = (ph, g, k - 1)
        here = full.at[ph, g, pl.ds(y * wide, wide)]
        return remote(here, here, agy_ss.at[i], agy_rs.at[i], y_peer(k))

    def got_agy(ph, g, k):
        i = (ph, g, k - 1)
        there = full.at[ph, g, pl.ds(lax.rem(y + n1 - k, n1) * wide, wide)]
        return remote(there, there, agy_ss.at[i], agy_rs.at[i], y_peer(k))

    def halo_down(src, halo, i):
        return remote(
            src.at[rows - 1], halo.at[0], halo_ss.at[i], halo_rs.at[i], {"space": s + 1}
        )

    def halo_up(src, halo, i):
        return remote(src.at[0], halo.at[1], halo_ss.at[i], halo_rs.at[i], {"space": s - 1})

    def start_halo(src, halo, i):
        @pl.when(s < n - 1)
        def _():
            halo_down(src, halo, i).start()

        @pl.when(s > 0)
        def _():
            halo_up(src, halo, i + 1).start()

    def wait_halo(src, halo, i):
        @pl.when(s > 0)
        def _():
            halo_down(src, halo, i).wait_recv()

        @pl.when(s == 0)
        def _():
            halo[0] = jnp.zeros((cols, width), BF)

        @pl.when(s < n - 1)
        def _():
            halo_up(src, halo, i + 1).wait_recv()

        @pl.when(s == n - 1)
        def _():
            halo[1] = jnp.zeros((cols, width), BF)

    def drain_halo(src, halo, i):
        @pl.when(s < n - 1)
        def _():
            halo_down(src, halo, i).wait_send()

        @pl.when(s > 0)
        def _():
            halo_up(src, halo, i + 1).wait_send()

    def keys_step(g):
        for j in range(GROUP):
            h = g * GROUP + j
            kx[h] = jnp.maximum(flat(k_ref, columns(h)), 0)
            vx[h] = ones_column
            vx[h, :, :HD] = flat(v_ref, columns(h))
            put_state(0, g, j, dot_tn(kx[h], vx[h]))
        pad_state(0, g)

    def query_step(g):
        for j in range(GROUP):
            h = g * GROUP + j
            state = full[0, g, j * HD:(j + 1) * HD]
            query = jnp.maximum(flat(q_ref, columns(h)), 0)
            gx[h] = zero_block
            gx[h, :, :HD] = flat(g_ref, columns(h))
            grad = gx[h].astype(F32)
            numerator = dot_nn(query, state)
            inverse = 1.0 / (numerator[:, HD:HD + 1] + 1.0)
            den_grad = -jnp.sum(grad * numerator, axis=1, keepdims=True) * (inverse * inverse)
            num_grad = jnp.where(lane == HD, den_grad, grad * inverse).astype(BF)
            att32[:, columns(h)] = (numerator * inverse)[:, :HD]
            gq32[:, columns(h)] = dot_nt(num_grad, state)
            put_state(1, g, j, dot_tn(query, num_grad))
        pad_state(1, g)

    def last_step(g):
        for j in range(GROUP):
            h = g * GROUP + j
            state = full[1, g, j * HD:(j + 1) * HD]
            gk32[:, columns(h)] = dot_nt(vx[h], state)
            gv32[:, columns(h)] = dot_nn(kx[h], state)[:, :HD]

    def send_rs1(ph, g):
        for k in range(1, n1):
            copy_rs1(ph, g, k).start()

    def step_rs2(ph, g):
        total = st32[ph, g, pl.ds(y * wide, wide)]
        for k in range(1, n1):
            copy_rs1(ph, g, k).wait_recv()
            total = total + rs1[ph, g, k - 1].astype(F32)
        a32[ph, g] = total
        a16[ph, g] = total.astype(BF)
        for k in range(1, n2):
            copy_rs2(ph, g, k).start()

    def step_pc(ph, g):
        total = a32[ph, g, pl.ds(x * chunk, chunk)]
        for k in range(1, n2):
            copy_rs2(ph, g, k).wait_recv()
            total = total + rs2[ph, g, k - 1].astype(F32)
        if ph == 1:
            total = total * inv_count
        p32[ph, g] = total
        copy_pc(ph, g).start()

    def step_z(ph, g):
        copy_pc(ph, g).wait_recv()
        t16[ph, g] = (p32[ph, g] + pc[ph, g]).astype(BF)
        for k in range(1, nz):
            @pl.when(z_sends(ph, k))
            def _():
                copy_zr(ph, g, k).start()

    def step_agx(ph, g):
        with_pair = core if ph == 0 else 1 - core
        a32[ph, g, :chunk] = p32[ph, g] + pc[ph, g] * with_pair.astype(F32)
        for k in range(1, nz):
            @pl.when(z_gets(ph, k))
            def _():
                copy_zr(ph, g, k).wait_recv()
                a32[ph, g, :chunk] += zr[ph, g, k - 1].astype(F32)
        total = a32[ph, g, :chunk]
        if ph == 0:
            total = total * inv_count
        full[ph, g, pl.ds(s * chunk, chunk)] = total.astype(BF)
        for k in range(1, n2):
            copy_agx(ph, g, k).start()

    def step_agy(ph, g):
        for k in range(1, n2):
            got_agx(ph, g, k).wait_recv()
        for k in range(1, n1):
            copy_agy(ph, g, k).start()

    def step_full(ph, g):
        for k in range(1, n1):
            got_agy(ph, g, k).wait_recv()

    def chain(step, g):
        if step == 0:
            keys_step(g)
            send_rs1(0, g)
        elif step == 6:
            step_full(0, g)
            query_step(g)
            send_rs1(1, g)
        elif step == 12:
            step_full(1, g)
            last_step(g)
        else:
            ph = 0 if step < 6 else 1
            (step_rs2, step_pc, step_z, step_agx, step_agy)[(step - 1) % 6](ph, g)

    col = lax.broadcasted_iota(jnp.int32, (tokens, 1), 0) % cols

    def filtered(src, halo, where, back):
        above = halo[0:1, :, where].astype(F32)
        here = src[:, :, where].astype(F32)
        below = halo[1:2, :, where].astype(F32)
        stack = jnp.concatenate([above, here, below], axis=0)
        sums = [None] * 3
        for a in range(3):
            weights = w_ref[a, :, where].astype(F32)
            first = 2 - a if back else a
            block = stack[first:first + rows].reshape(tokens, -1)
            for b in range(3):
                term = weights[b:b + 1] * block
                sums[b] = term if sums[b] is None else sums[b] + term
        left, right = (sums[2], sums[0]) if back else (sums[0], sums[2])
        left = jnp.where(col == 0, 0.0, pltpu.roll(left, 1, 0))
        right = jnp.where(col == cols - 1, 0.0, pltpu.roll(right, tokens - 1, 0))
        return sums[1] + left + right

    def over_lanes(body):
        whole = width // LANES

        @pl.loop(0, whole)
        def _(i):
            body(pl.ds(pl.multiple_of(i * LANES, LANES), LANES), LANES)

        if width % LANES:
            body(slice(whole * LANES, width), width % LANES)

    def shaped(block, size):
        return block.reshape(rows, cols, size)

    def finish_forward(where, size):
        block = att32[:, where] + filtered(v_ref, halo_v, where, False)
        att_ref[:, :, where] = shaped(block.astype(BF), size)
        queries = flat(q_ref, where).astype(F32)
        grads = jnp.where(queries > 0, gq32[:, where], 0.0)
        gq_ref[:, :, where] = shaped(grads.astype(BF), size)

    def conv_grads(where, size):
        att32[:, where] = filtered(g_ref, halo_g, where, True)

    def finish_backward(where, size):
        keys = flat(k_ref, where).astype(F32)
        grads = jnp.where(keys > 0, gk32[:, where], 0.0)
        gk_ref[:, :, where] = shaped(grads.astype(BF), size)
        gv_ref[:, :, where] = shaped((gv32[:, where] + att32[:, where]).astype(BF), size)

    fan = (n1 - 1) + (n2 - 1) + 1 + (nz - 1)
    pl.semaphore_wait(
        barrier, fan + jnp.where(s > 0, 1, 0) + jnp.where(s < n - 1, 1, 0)
    )

    start_halo(v_ref, halo_v, 0)
    for tick in range(12 + GROUPS):
        for g in range(GROUPS):
            step = tick - g
            if 0 <= step <= 12:
                chain(step, g)
        if tick == 4:
            start_halo(g_ref, halo_g, 2)
        if tick == 5 + GROUPS:
            wait_halo(v_ref, halo_v, 0)
            over_lanes(finish_forward)
            wait_halo(g_ref, halo_g, 2)
            over_lanes(conv_grads)
    over_lanes(finish_backward)

    drain_halo(v_ref, halo_v, 0)
    drain_halo(g_ref, halo_g, 2)
    for ph in range(2):
        for g in range(GROUPS):
            for k in range(1, n1):
                copy_rs1(ph, g, k).wait_send()
                copy_agy(ph, g, k).wait_send()
            for k in range(1, n2):
                copy_rs2(ph, g, k).wait_send()
                copy_agx(ph, g, k).wait_send()
            copy_pc(ph, g).wait_send()
            for k in range(1, nz):
                @pl.when(z_sends(ph, k))
                def _():
                    copy_zr(ph, g, k).wait_send()


def factors(n):
    first = math.isqrt(n)
    while n % first:
        first -= 1
    return first, n // first


def on_device(nz, n1, n2, queries, keys_in, values, conv_weight, grad_out):
    _, rows, cols, width = queries.shape
    tokens = rows * cols
    n = n1 * n2
    chunk = -(-GROUP * HD // (16 * n)) * 16
    shape3 = (rows, cols, width)
    vmem = pl.BlockSpec(memory_space=pltpu.VMEM)

    def dma(*shape):
        return pltpu.SemaphoreType.DMA(tuple(max(1, e) for e in shape))

    def buf(shape, dtype):
        return pltpu.VMEM(tuple(max(1, e) for e in shape), dtype)

    lead = (2, GROUPS)
    sems = [dma(4), dma(4)]
    for tail in ((n1 - 1,), (n2 - 1,), (), (nz - 1,), (n2 - 1,), (n1 - 1,)):
        sems += [dma(*lead, *tail), dma(*lead, *tail)]
    outs = pl.pallas_call(
        functools.partial(kernel, nz, n1, n2, chunk),
        out_shape=[jax.ShapeDtypeStruct(shape3, BF)] * 4,
        in_specs=[vmem] * 5,
        out_specs=[vmem] * 4,
        scratch_shapes=[
            buf((HEADS, tokens, LANES), BF),
            buf((HEADS, tokens, HD), BF),
            buf((HEADS, tokens, LANES), BF),
            buf((tokens, width), F32),
            buf((tokens, width), F32),
            buf((tokens, width), F32),
            buf((tokens, width), F32),
            buf((2, cols, width), BF),
            buf((2, cols, width), BF),
            buf((*lead, n * chunk, LANES), F32),
            buf((*lead, n * chunk, LANES), BF),
            buf((*lead, n2 * chunk, LANES), F32),
            buf((*lead, n2 * chunk, LANES), BF),
            buf((*lead, chunk, LANES), F32),
            buf((*lead, chunk, LANES), BF),
            buf((*lead, n1 - 1, n2 * chunk, LANES), BF),
            buf((*lead, n2 - 1, chunk, LANES), BF),
            buf((*lead, chunk, LANES), F32),
            buf((*lead, nz - 1, chunk, LANES), BF),
            buf((*lead, n * chunk, LANES), BF),
            *sems,
        ],
        compiler_params=pltpu.CompilerParams(
            collective_id=0, has_side_effects=True, vmem_limit_bytes=48 * 2**20
        ),
    )(
        queries.reshape(shape3), keys_in.reshape(shape3), values.reshape(shape3),
        conv_weight, grad_out.reshape(shape3),
    )
    return tuple(o.reshape(queries.shape) for o in outs)


def solution(mesh):
    nz = mesh.shape["orbit"] // 2
    n1, n2 = factors(mesh.shape["space"])
    field = P("orbit", "space", None, None)
    return jax.shard_map(
        functools.partial(on_device, nz, n1, n2),
        mesh=mesh,
        in_specs=(field, field, field, P(), field),
        out_specs=(field, field, field, field),
        check_vma=False,
    )
```

```python
import functools
import math

import jax
import jax.numpy as jnp
from jax import lax
from jax.experimental import pallas as pl
from jax.experimental.pallas import tpu as pltpu
from jax.sharding import PartitionSpec as P

HEADS = 20
HD = 112
LANES = 128
GROUP = 4
GROUPS = HEADS // GROUP
PIECE = 16
VALUE_HALO = 0
GRAD_HALO = 5
QUERY_TICK = 6
FORWARD_TICK = 8
CONV_TICK = 11
BF = jnp.bfloat16
F32 = jnp.float32
MESH = pl.DeviceIdType.MESH


def dot_tn(a, b):
    return lax.dot_general(a, b, (((0,), (0,)), ((), ())), preferred_element_type=F32)


def dot_nt(a, b):
    return lax.dot_general(a, b, (((1,), (1,)), ((), ())), preferred_element_type=F32)


def dot_nn(a, b):
    return lax.dot_general(a, b, (((1,), (0,)), ((), ())), preferred_element_type=F32)


def kernel(
    nz, n1, n2, chunk,
    q_hbm, k_hbm, v_hbm, w_hbm, g_hbm,
    att_ref, gq_ref, gk_ref, gv_ref,
    q_ref, k_ref, v_ref, w_ref, g_ref, in_sems,
    vx, kx, gx, att32, gq32, gk32, gv32, conv32, halo_v, halo_g,
    st32, st16, a32, a16, p32, t16, rs1, rs2, pc, zr, full,
    halo_ss, halo_rs, rs1_ss, rs1_rs, rs2_ss, rs2_rs, pc_ss, pc_rs, zr_ss, zr_rs,
    agx_ss, agx_rs, agy_ss, agy_rs,
):
    rows, cols, width = v_ref.shape
    tokens = rows * cols
    n = n1 * n2
    wide = n2 * chunk
    group_rows = GROUP * HD
    u = lax.axis_index("orbit")
    s = lax.axis_index("space")
    z, core = u // 2, u % 2
    y, x = s // n2, s % n2
    count = (u + 1).astype(F32) * float(rows * n * cols)
    inv_count = 1.0 / count
    pair = z * 2 + (1 - core)

    def y_peer(k):
        return {"space": lax.rem(y + k, n1) * n2 + x}

    def x_peer(k):
        return {"space": y * n2 + lax.rem(x + k, n2)}

    def z_peer(k):
        return {"orbit": (z + k) * 2 + core}

    barrier = pltpu.get_barrier_semaphore()
    for k in range(1, n1):
        pl.semaphore_signal(barrier, inc=1, device_id=y_peer(k), device_id_type=MESH)
    for k in range(1, n2):
        pl.semaphore_signal(barrier, inc=1, device_id=x_peer(k), device_id_type=MESH)
    pl.semaphore_signal(barrier, inc=1, device_id={"orbit": pair}, device_id_type=MESH)
    for k in range(1, nz):
        pl.semaphore_signal(
            barrier, inc=1, device_id={"orbit": lax.rem(z + k, nz) * 2 + core},
            device_id_type=MESH,
        )

    @pl.when(s > 0)
    def _():
        pl.semaphore_signal(barrier, inc=1, device_id={"space": s - 1}, device_id_type=MESH)

    @pl.when(s < n - 1)
    def _():
        pl.semaphore_signal(barrier, inc=1, device_id={"space": s + 1}, device_id_type=MESH)

    loads = [
        pltpu.make_async_copy(src, dst, in_sems.at[i])
        for i, (src, dst) in enumerate(
            ((k_hbm, k_ref), (v_hbm, v_ref), (g_hbm, g_ref), (q_hbm, q_ref), (w_hbm, w_ref))
        )
    ]
    for load in loads:
        load.start()

    lane = lax.broadcasted_iota(jnp.int32, (tokens, LANES), 1)
    ones_column = jnp.where(lane == HD, 1.0, 0.0).astype(BF)
    zero_block = jnp.zeros((tokens, LANES), BF)

    def columns(h):
        return slice(h * HD, (h + 1) * HD)

    def flat(ref, where):
        return ref[:, :, where].reshape(tokens, -1)

    def put_state(ph, g, j, block):
        st32[ph, g, j * HD:(j + 1) * HD] = block
        st16[ph, g, j * HD:(j + 1) * HD] = block.astype(BF)

    def pad_state(ph, g):
        if n * chunk > group_rows:
            extra = n * chunk - group_rows
            st32[ph, g, group_rows:] = jnp.zeros((extra, LANES), F32)
            st16[ph, g, group_rows:] = jnp.zeros((extra, LANES), BF)

    def remote(src, dst, ss, rs, to):
        return pltpu.make_async_remote_copy(
            src_ref=src, dst_ref=dst, send_sem=ss, recv_sem=rs,
            device_id=to, device_id_type=MESH,
        )

    def copy_rs1(ph, g, k):
        part = st16.at[ph, g, pl.ds(lax.rem(y + k, n1) * wide, wide)]
        i = (ph, g, k - 1)
        return remote(part, rs1.at[i], rs1_ss.at[i], rs1_rs.at[i], y_peer(k))

    def copy_rs2(ph, g, k):
        part = a16.at[ph, g, pl.ds(lax.rem(x + k, n2) * chunk, chunk)]
        i = (ph, g, k - 1)
        return remote(part, rs2.at[i], rs2_ss.at[i], rs2_rs.at[i], x_peer(k))

    def copy_pc(ph, g):
        i = (ph, g)
        return remote(p32.at[i], pc.at[i], pc_ss.at[i], pc_rs.at[i], {"orbit": pair})

    def copy_zr(ph, g, k):
        i = (ph, g, k - 1)
        return remote(
            t16.at[ph, g], zr.at[i], zr_ss.at[i], zr_rs.at[i], z_peer(k if ph == 0 else -k)
        )

    def z_sends(ph, k):
        return (z + k < nz) if ph == 0 else (z - k >= 0)

    def z_gets(ph, k):
        return (z - k >= 0) if ph == 0 else (z + k < nz)

    def copy_agx(ph, g, k):
        i = (ph, g, k - 1)
        here = full.at[ph, g, pl.ds(s * chunk, chunk)]
        return remote(here, here, agx_ss.at[i], agx_rs.at[i], x_peer(k))

    def got_agx(ph, g, k):
        i = (ph, g, k - 1)
        there = full.at[ph, g, pl.ds((y * n2 + lax.rem(x + n2 - k, n2)) * chunk, chunk)]
        return remote(there, there, agx_ss.at[i], agx_rs.at[i], x_peer(k))

    def copy_agy(ph, g, k):
        i = (ph, g, k - 1)
        here = full.at[ph, g, pl.ds(y * wide, wide)]
        return remote(here, here, agy_ss.at[i], agy_rs.at[i], y_peer(k))

    def got_agy(ph, g, k):
        i = (ph, g, k - 1)
        there = full.at[ph, g, pl.ds(lax.rem(y + n1 - k, n1) * wide, wide)]
        return remote(there, there, agy_ss.at[i], agy_rs.at[i], y_peer(k))

    pieces = cols // PIECE

    def halo_down(src, halo, i, p):
        part = pl.ds(p * PIECE, PIECE)
        return remote(
            src.at[rows - 1, part], halo.at[0, part], halo_ss.at[i, p], halo_rs.at[i, p],
            {"space": s + 1},
        )

    def halo_up(src, halo, i, p):
        part = pl.ds(p * PIECE, PIECE)
        return remote(
            src.at[0, part], halo.at[1, part], halo_ss.at[i + 1, p], halo_rs.at[i + 1, p],
            {"space": s - 1},
        )

    def start_halo(src, halo, i, p):
        @pl.when(s < n - 1)
        def _():
            halo_down(src, halo, i, p).start()

        @pl.when(s > 0)
        def _():
            halo_up(src, halo, i, p).start()

    def wait_halo(src, halo, i):
        @pl.when(s > 0)
        def _():
            for p in range(pieces):
                halo_down(src, halo, i, p).wait_recv()

        @pl.when(s == 0)
        def _():
            halo[0] = jnp.zeros((cols, width), BF)

        @pl.when(s < n - 1)
        def _():
            for p in range(pieces):
                halo_up(src, halo, i, p).wait_recv()

        @pl.when(s == n - 1)
        def _():
            halo[1] = jnp.zeros((cols, width), BF)

    def drain_halo(src, halo, i):
        @pl.when(s < n - 1)
        def _():
            for p in range(pieces):
                halo_down(src, halo, i, p).wait_send()

        @pl.when(s > 0)
        def _():
            for p in range(pieces):
                halo_up(src, halo, i, p).wait_send()

    def keys_step(g):
        for j in range(GROUP):
            h = g * GROUP + j
            kx[h] = jnp.maximum(flat(k_ref, columns(h)), 0)
            vx[h] = ones_column
            vx[h, :, :HD] = flat(v_ref, columns(h))
            put_state(0, g, j, dot_tn(kx[h], vx[h]))
        pad_state(0, g)

    def query_step(g):
        for j in range(GROUP):
            h = g * GROUP + j
            state = full[0, g, j * HD:(j + 1) * HD]
            query = jnp.maximum(flat(q_ref, columns(h)), 0)
            gx[h] = zero_block
            gx[h, :, :HD] = flat(g_ref, columns(h))
            grad = gx[h].astype(F32)
            numerator = dot_nn(query, state)
            inverse = 1.0 / (numerator[:, HD:HD + 1] + 1.0)
            den_grad = -jnp.sum(grad * numerator, axis=1, keepdims=True) * (inverse * inverse)
            num_grad = jnp.where(lane == HD, den_grad, grad * inverse).astype(BF)
            att32[:, columns(h)] = (numerator * inverse)[:, :HD]
            gq32[:, columns(h)] = dot_nt(num_grad, state)
            put_state(1, g, j, dot_tn(query, num_grad))
        pad_state(1, g)

    def last_step(g):
        for j in range(GROUP):
            h = g * GROUP + j
            state = full[1, g, j * HD:(j + 1) * HD]
            gk32[:, columns(h)] = dot_nt(vx[h], state)
            gv32[:, columns(h)] = dot_nn(kx[h], state)[:, :HD]

    def send_rs1(ph, g):
        for k in range(1, n1):
            copy_rs1(ph, g, k).start()

    def step_rs2(ph, g):
        total = st32[ph, g, pl.ds(y * wide, wide)]
        for k in range(1, n1):
            copy_rs1(ph, g, k).wait_recv()
            total = total + rs1[ph, g, k - 1].astype(F32)
        a32[ph, g] = total
        a16[ph, g] = total.astype(BF)
        for k in range(1, n2):
            copy_rs2(ph, g, k).start()

    def step_pc(ph, g):
        total = a32[ph, g, pl.ds(x * chunk, chunk)]
        for k in range(1, n2):
            copy_rs2(ph, g, k).wait_recv()
            total = total + rs2[ph, g, k - 1].astype(F32)
        if ph == 1:
            total = total * inv_count
        p32[ph, g] = total
        copy_pc(ph, g).start()

    def step_z(ph, g):
        copy_pc(ph, g).wait_recv()
        t16[ph, g] = (p32[ph, g] + pc[ph, g]).astype(BF)
        for k in range(1, nz):
            @pl.when(z_sends(ph, k))
            def _():
                copy_zr(ph, g, k).start()

    def step_agx(ph, g):
        with_pair = core if ph == 0 else 1 - core
        a32[ph, g, :chunk] = p32[ph, g] + pc[ph, g] * with_pair.astype(F32)
        for k in range(1, nz):
            @pl.when(z_gets(ph, k))
            def _():
                copy_zr(ph, g, k).wait_recv()
                a32[ph, g, :chunk] += zr[ph, g, k - 1].astype(F32)
        total = a32[ph, g, :chunk]
        if ph == 0:
            total = total * inv_count
        full[ph, g, pl.ds(s * chunk, chunk)] = total.astype(BF)
        for k in range(1, n2):
            copy_agx(ph, g, k).start()

    def step_agy(ph, g):
        for k in range(1, n2):
            got_agx(ph, g, k).wait_recv()
        for k in range(1, n1):
            copy_agy(ph, g, k).start()

    def step_full(ph, g):
        for k in range(1, n1):
            got_agy(ph, g, k).wait_recv()

    def chain(step, g):
        if step == 0:
            if g:
                keys_step(g)
            send_rs1(0, g)
        elif step == 6:
            step_full(0, g)
            query_step(g)
            send_rs1(1, g)
        elif step == 12:
            step_full(1, g)
            last_step(g)
        else:
            ph = 0 if step < 6 else 1
            (step_rs2, step_pc, step_z, step_agx, step_agy)[(step - 1) % 6](ph, g)

    col = lax.broadcasted_iota(jnp.int32, (tokens, 1), 0) % cols

    def filtered(src, halo, where, back):
        above = halo[0:1, :, where].astype(F32)
        here = src[:, :, where].astype(F32)
        below = halo[1:2, :, where].astype(F32)
        stack = jnp.concatenate([above, here, below], axis=0)
        sums = [None] * 3
        for a in range(3):
            weights = w_ref[a, :, where].astype(F32)
            first = 2 - a if back else a
            block = stack[first:first + rows].reshape(tokens, -1)
            for b in range(3):
                term = weights[b:b + 1] * block
                sums[b] = term if sums[b] is None else sums[b] + term
        left, right = (sums[2], sums[0]) if back else (sums[0], sums[2])
        left = jnp.where(col == 0, 0.0, pltpu.roll(left, 1, 0))
        right = jnp.where(col == cols - 1, 0.0, pltpu.roll(right, tokens - 1, 0))
        return sums[1] + left + right

    def over_lanes(body, g):
        first = g * group_rows // LANES
        last = (g + 1) * group_rows // LANES

        @pl.loop(first, last)
        def _(i):
            body(pl.ds(pl.multiple_of(i * LANES, LANES), LANES), LANES)

        if g == GROUPS - 1 and width % LANES:
            body(slice(last * LANES, width), width % LANES)

    def shaped(block, size):
        return block.reshape(rows, cols, size)

    def finish_forward(where, size):
        block = att32[:, where] + filtered(v_ref, halo_v, where, False)
        att_ref[:, :, where] = shaped(block.astype(BF), size)
        queries = flat(q_ref, where).astype(F32)
        grads = jnp.where(queries > 0, gq32[:, where], 0.0)
        gq_ref[:, :, where] = shaped(grads.astype(BF), size)

    def conv_grads(where, size):
        conv32[:, where] = filtered(g_ref, halo_g, where, True)

    def finish_backward(where, size):
        keys = flat(k_ref, where).astype(F32)
        grads = jnp.where(keys > 0, gk32[:, where], 0.0)
        gk_ref[:, :, where] = shaped(grads.astype(BF), size)
        gv_ref[:, :, where] = shaped((gv32[:, where] + conv32[:, where]).astype(BF), size)

    for load in loads[:2]:
        load.wait()
    keys_step(0)
    fan = (n1 - 1) + (n2 - 1) + 1 + (nz - 1)
    pl.semaphore_wait(
        barrier, fan + jnp.where(s > 0, 1, 0) + jnp.where(s < n - 1, 1, 0)
    )

    for tick in range(12 + GROUPS):
        if tick == QUERY_TICK:
            loads[3].wait()
            loads[4].wait()
        if tick == GRAD_HALO:
            loads[2].wait()
        for g in range(GROUPS):
            step = tick - g
            if 0 <= step <= 12:
                chain(step, g)
        for p in range(pieces):
            if tick == VALUE_HALO + p:
                start_halo(v_ref, halo_v, 0, p)
            if tick == GRAD_HALO + p:
                start_halo(g_ref, halo_g, 2, p)
        g = tick - FORWARD_TICK
        if g == 0:
            wait_halo(v_ref, halo_v, 0)
        if 0 <= g < GROUPS:
            over_lanes(finish_forward, g)
        g = tick - CONV_TICK
        if g == 0:
            wait_halo(g_ref, halo_g, 2)
        if 0 <= g < GROUPS:
            over_lanes(conv_grads, g)
        g = tick - 12
        if 0 <= g < GROUPS:
            over_lanes(finish_backward, g)

    drain_halo(v_ref, halo_v, 0)
    drain_halo(g_ref, halo_g, 2)
    for ph in range(2):
        for g in range(GROUPS):
            for k in range(1, n1):
                copy_rs1(ph, g, k).wait_send()
                copy_agy(ph, g, k).wait_send()
            for k in range(1, n2):
                copy_rs2(ph, g, k).wait_send()
                copy_agx(ph, g, k).wait_send()
            copy_pc(ph, g).wait_send()
            for k in range(1, nz):
                @pl.when(z_sends(ph, k))
                def _():
                    copy_zr(ph, g, k).wait_send()


def factors(n):
    first = math.isqrt(n)
    while n % first:
        first -= 1
    return first, n // first


def on_device(nz, n1, n2, queries, keys_in, values, conv_weight, grad_out):
    _, rows, cols, width = queries.shape
    tokens = rows * cols
    n = n1 * n2
    chunk = -(-GROUP * HD // (16 * n)) * 16
    shape3 = (rows, cols, width)
    vmem = pl.BlockSpec(memory_space=pltpu.VMEM)

    def dma(*shape):
        return pltpu.SemaphoreType.DMA(tuple(max(1, e) for e in shape))

    def buf(shape, dtype):
        return pltpu.VMEM(tuple(max(1, e) for e in shape), dtype)

    lead = (2, GROUPS)
    sems = [dma(4, cols // PIECE), dma(4, cols // PIECE)]
    for tail in ((n1 - 1,), (n2 - 1,), (), (nz - 1,), (n2 - 1,), (n1 - 1,)):
        sems += [dma(*lead, *tail), dma(*lead, *tail)]
    outs = pl.pallas_call(
        functools.partial(kernel, nz, n1, n2, chunk),
        out_shape=[jax.ShapeDtypeStruct(shape3, BF)] * 4,
        in_specs=[pl.BlockSpec(memory_space=pltpu.HBM)] * 5,
        out_specs=[vmem] * 4,
        scratch_shapes=[
            buf(shape3, BF), buf(shape3, BF), buf(shape3, BF), buf(conv_weight.shape, BF),
            buf(shape3, BF), dma(5),
            buf((HEADS, tokens, LANES), BF),
            buf((HEADS, tokens, HD), BF),
            buf((HEADS, tokens, LANES), BF),
            buf((tokens, width), F32),
            buf((tokens, width), F32),
            buf((tokens, width), F32),
            buf((tokens, width), F32),
            buf((tokens, width), F32),
            buf((2, cols, width), BF),
            buf((2, cols, width), BF),
            buf((*lead, n * chunk, LANES), F32),
            buf((*lead, n * chunk, LANES), BF),
            buf((*lead, n2 * chunk, LANES), F32),
            buf((*lead, n2 * chunk, LANES), BF),
            buf((*lead, chunk, LANES), F32),
            buf((*lead, chunk, LANES), BF),
            buf((*lead, n1 - 1, n2 * chunk, LANES), BF),
            buf((*lead, n2 - 1, chunk, LANES), BF),
            buf((*lead, chunk, LANES), F32),
            buf((*lead, nz - 1, chunk, LANES), BF),
            buf((*lead, n * chunk, LANES), BF),
            *sems,
        ],
        compiler_params=pltpu.CompilerParams(
            collective_id=0, has_side_effects=True, vmem_limit_bytes=48 * 2**20
        ),
    )(
        queries.reshape(shape3), keys_in.reshape(shape3), values.reshape(shape3),
        conv_weight, grad_out.reshape(shape3),
    )
    return tuple(o.reshape(queries.shape) for o in outs)


def solution(mesh):
    nz = mesh.shape["orbit"] // 2
    n1, n2 = factors(mesh.shape["space"])
    field = P("orbit", "space", None, None)
    return jax.shard_map(
        functools.partial(on_device, nz, n1, n2),
        mesh=mesh,
        in_specs=(field, field, field, P(), field),
        out_specs=(field, field, field, field),
        check_vma=False,
    )
```
